1024 devices in a mesh: dp: 32 (over y, x_hi, core), expert: 32 (over x_lo, z).
Axes of the slice: x: 4 (x_hi: 2, x_lo: 2; x = x_hi * 2 + x_lo), y: 8, z: 16, core: 2. Of those that a mesh axis runs over, the one named last changes fastest.
Arguments:
- cotangent: bfloat16 [131072, 3584], P(('dp', 'expert')), may hold values from -6 to 6
- gates: bfloat16 [131072, 1], P(('dp', 'expert')), may hold values from 0.049804688 to 1
- expert_ids: int32 [131072, 1], P(('dp', 'expert')), may hold values from 0 to 63; in each aligned block of 128 rows (0 to 127, 128 to 255, ...) at most 3 rows name the same one
- hidden: bfloat16 [32, 64, 32, 3, 2560], P('dp', 'expert'), may hold values from -6 to 6
- factor_a: bfloat16 [64, 2560, 128], P('expert'), may hold values from -0.125 to 0.125
- factor_b: bfloat16 [64, 128, 3584], P('expert'), may hold values from -0.5 to 0.5
Outputs:
- grad_a: float32 [64, 2560, 128], P('expert', 'dp')
- grad_b: float32 [64, 128, 3584], P('expert', None, 'dp')
- grad_hidden: bfloat16 [32, 64, 32, 3, 2560], P('dp', 'expert')
- grad_gates: float32 [131072, 1], P(('dp', 'expert'))
The draws below stay inside these ranges and needn't reach their ends.
Inputs may be any that keep to these rules, and one draw needn't show every extreme that they name: `expert_ids`: among the 128 tokens of one device no expert is named more than 3 times, a bound that some block reaches.
All inputs are finite; a program needn't handle non-finite values.
Results may differ from the reference program's by a relative error of at most 0.0057.
Values may be sent and summed in bfloat16 or wider, within the bound.
No kernel may reach another device: no remote copies, remote signals or barrier semaphores. Data moves between devices by JAX's collectives and lax.ppermute only.
A program may use at most 64 MiB of HBM per device.

```python
import math
import jax
import jax.numpy as jnp
import numpy as np
from jax import lax

D = 3584
F = 2560
R = 128
TOK_DEV = 128
TOP = 1
EXPERT_COUNT = 64
EXPERT_CAPACITY = 3
TOKENS = 131072
N_DP = 32
N_EXPERT = 32


def block_levels(key, dims, pieces, low, high):
    level, own = 1.0, jax.random.fold_in(key, 6)
    for position, shards_of in pieces:
        draws = jnp.exp(jax.random.uniform(jax.random.fold_in(own, position), (shards_of,), jnp.float32, low / len(pieces), high / len(pieces)))
        level = level * jnp.repeat(draws, dims[position] // shards_of).reshape([-1 if axis == position else 1 for axis in range(len(dims))])
    return level


def deal_out(rng, own, number, rows, count, top, most, slope):
    sequence = jax.random.permutation(rng, count)
    heavy_load, ordinary = load_shares(count, rows * top, most, slope, True), load_shares(count, rows * top, most, slope, False)
    places = jnp.arange(count)

    def named(lengths, rotation):
        used = int((lengths > 0).sum())
        fixed = max(1, used // 4)
        passed = fixed + (places - fixed + rotation * (used - fixed)) % max(1, count - fixed)
        return jnp.zeros((count,), jnp.int32).at[sequence[jnp.where(places < fixed, places, passed)]].set(jnp.asarray(lengths, jnp.int32))

    lengths = jnp.where(number % 4 == 0, named(heavy_load, number // 4), named(ordinary, number - number // 4 - 1))
    mixed = jax.random.permutation(jax.random.fold_in(own, 3), count)
    donor, taker = mixed[0:count // 2 * 2:2], mixed[1:count // 2 * 2:2]
    slack = jnp.minimum(lengths[donor] - 1, most - lengths[taker]) // 2
    slack = jnp.where((donor == sequence[0]) | (taker == sequence[0]) | (lengths[taker] == 0), 0, jnp.maximum(slack, 0))
    passed = jax.random.randint(jax.random.fold_in(own, 4), (count // 2,), 0, 1 << 20) % (slack + 1)
    lengths = lengths.at[donor].add(-passed).at[taker].add(passed)
    items = jnp.searchsorted(jnp.cumsum(lengths), jnp.arange(rows * top), side="right").astype(jnp.int32)
    grid = items.reshape(top, rows).T
    grid = grid[jax.random.permutation(jax.random.fold_in(own, 1), rows)]
    rotation = jax.random.randint(jax.random.fold_in(own, 2), (rows, 1), 0, top)
    return jnp.take_along_axis(grid, (jnp.arange(top)[None, :] + rotation) % top, axis=1)


def load_shares(number_of, total, reach, lean, full):
    portions = [(1 << 20) // math.isqrt(standing ** lean) + 1 for standing in range(1, number_of + 1)]
    largest = reach if full else min(reach, max(-(-total // number_of), total * portions[0] // sum(portions)))
    least = 1 if total - largest >= number_of - 1 else 0
    counts, spare = [largest] + [least] * (number_of - 1), total - largest - least * (number_of - 1)
    while spare > 0:
        candidates = [i for i in range(1, number_of) if counts[i] < largest] or [i for i in range(1, number_of) if counts[i] < reach]
        whole, left = sum([portions[i] for i in candidates]), spare
        for i in candidates:
            more = min(reach - counts[i], max(1, left * portions[i] // whole), spare)
            counts[i] = counts[i] + more
            spare = spare - more
    return np.array(counts)


def gaussian(key, shape, spread, most, shards=(), kind=jnp.bfloat16):
    gain = block_levels(key, shape, shards, -0.22, 0.18) if shards else 1.0
    values = jax.random.normal(key, shape, jnp.float32) * spread * gain
    return jnp.minimum(jnp.maximum(values, -most), most).astype(kind)


def setup_inputs(seed: int = 0) -> dict:
    seeds = jax.random.split(jax.random.key(seed), 7)
    cotangent = gaussian(seeds[0], (TOKENS, D), 1.0, 6.0, ((0, 1024),))
    gates = jnp.clip(0.049804688 + 0.9501953 * jax.random.uniform(seeds[1], (TOKENS, TOP), jnp.float32) ** block_levels(seeds[1], (TOKENS, TOP), ((0, 1024),), -0.2, 0.2), 0.049804688, 1.0).astype(jnp.bfloat16)
    expert_ids_keys = jax.random.split(jax.random.fold_in(seeds[2], 1), TOKENS // TOK_DEV)
    expert_ids_turns = jax.random.permutation(jax.random.fold_in(seeds[2], 3), TOKENS // TOK_DEV)
    expert_ids = jax.vmap(lambda own, number: deal_out(jax.random.fold_in(seeds[2], 2), own, number, TOK_DEV, EXPERT_COUNT, TOP, EXPERT_CAPACITY, 2))(expert_ids_keys, expert_ids_turns).reshape((TOKENS, TOP))
    hidden = gaussian(seeds[3], (N_DP, EXPERT_COUNT, N_EXPERT, EXPERT_CAPACITY, F), 1.0, 6.0, ((0, 32), (1, 32)))
    factor_a = gaussian(seeds[4], (EXPERT_COUNT, F, R), F ** -0.5, 0.125, ((0, 32),))
    factor_b = gaussian(seeds[5], (EXPERT_COUNT, R, D), R ** -0.5, 0.5, ((0, 32),))
    return {"cotangent": cotangent, "gates": gates, "expert_ids": expert_ids, "hidden": hidden, "factor_a": factor_a, "factor_b": factor_b}


def reference(cotangent, gates, expert_ids, hidden, factor_a, factor_b):
    pairs = TOK_DEV * TOP
    dy_all = cotangent.reshape(N_DP, N_EXPERT, TOK_DEV, D)
    gate_all = gates.reshape(N_DP, N_EXPERT, pairs)
    ids_all = expert_ids.reshape(N_DP, N_EXPERT, pairs)
    fa = factor_a.astype(jnp.float32)
    fb = factor_b.astype(jnp.float32)

    def group(carry, inputs):
        dy_p, gate_portion, ids_p, hid_p = inputs
        onehot = (ids_p[:, :, None] == jnp.arange(EXPERT_COUNT, dtype=jnp.int32)[None, None, :]).astype(jnp.int32)
        rank = jnp.sum((jnp.cumsum(onehot, axis=1) - onehot) * onehot, axis=2).astype(jnp.int32)
        slot_position = (ids_p * EXPERT_CAPACITY + rank).astype(jnp.int32)
        rows = jnp.repeat(dy_p, TOP, axis=1)
        source_token = jnp.arange(N_EXPERT, dtype=jnp.int32)[:, None]
        slot_buffer = jnp.zeros((N_EXPERT, EXPERT_COUNT * EXPERT_CAPACITY, D), jnp.bfloat16).at[source_token, slot_position].set(rows)
        gradient_buffer = jnp.zeros((N_EXPERT, EXPERT_COUNT * EXPERT_CAPACITY), jnp.float32).at[source_token, slot_position].set(gate_portion.astype(jnp.float32))
        slot_output_gradient = (gradient_buffer[:, :, None] * slot_buffer.astype(jnp.float32)).astype(jnp.bfloat16)
        slot_output_gradient = jnp.transpose(slot_output_gradient.reshape(N_EXPERT, EXPERT_COUNT, EXPERT_CAPACITY, D), (1, 0, 2, 3)).astype(jnp.float32)
        slot_dy = jnp.transpose(slot_buffer.reshape(N_EXPERT, EXPERT_COUNT, EXPERT_CAPACITY, D), (1, 0, 2, 3)).astype(jnp.float32)
        hid = hid_p.astype(jnp.float32)
        low = jnp.einsum('escf,efr->escr', hid, fa).astype(jnp.bfloat16).astype(jnp.float32)
        grad_low = jnp.einsum('escd,erd->escr', slot_output_gradient, fb).astype(jnp.bfloat16).astype(jnp.float32)
        acc_a = carry[0] + jnp.einsum('escf,escr->efr', hid, grad_low)
        acc_b = carry[1] + jnp.einsum('escr,escd->erd', low, slot_output_gradient)
        grad_hid = jnp.einsum('escr,efr->escf', grad_low, fa).astype(jnp.bfloat16)
        slot_out = jnp.einsum('escr,erd->escd', low, fb)
        slot_gate = jnp.sum(slot_dy * slot_out, axis=3)
        slot_gate = jnp.transpose(slot_gate, (1, 0, 2)).reshape(N_EXPERT, EXPERT_COUNT * EXPERT_CAPACITY)
        grad_gate = jnp.take_along_axis(slot_gate, slot_position, axis=1)
        return (acc_a, acc_b), (grad_hid, grad_gate)

    init = (jnp.zeros((EXPERT_COUNT, F, R), jnp.float32), jnp.zeros((EXPERT_COUNT, R, D), jnp.float32))
    (grad_a, grad_b), (grad_hidden, grad_gates) = lax.scan(group, init, (dy_all, gate_all, ids_all, hidden))
    return grad_a, grad_b, grad_hidden, grad_gates.reshape(TOKENS, TOP)
```

```python
import jax
import jax.numpy as jnp
from jax import lax
from jax.experimental import pallas as pl
from jax.experimental.pallas import tpu as pltpu
from jax.sharding import Mesh, PartitionSpec as P

CAP = 3
ROWS = 4
SIDES = ("k", "expert")
GROUPS = ("q", "k")


def place_kernel(experts, ids_ref, gate_ref, part_ref, last_ref, send_ref, row_ref):
    tokens = ids_ref.shape[1]
    ids = ids_ref[...]
    expert = lax.broadcasted_iota(jnp.int32, (experts, tokens), 0)
    named = expert == ids
    older = lax.broadcasted_iota(jnp.int32, (tokens, tokens), 0)
    newer = lax.broadcasted_iota(jnp.int32, (tokens, tokens), 1)
    before = jnp.dot(
        named.astype(jnp.bfloat16),
        (older < newer).astype(jnp.bfloat16),
        preferred_element_type=jnp.float32,
    )
    rank = jnp.sum(jnp.where(named, before, 0.0), axis=0, keepdims=True).astype(jnp.int32)
    block = (ids % 2) * (experts // 2) + ids // 2
    row_ref[...] = block * ROWS + rank

    c = pl.program_id(0)
    row = lax.broadcasted_iota(jnp.int32, (experts * ROWS, tokens), 0)
    whole = row == block * ROWS + rank
    rest = (row == block * ROWS + CAP) & (rank == c)
    gate = jnp.sum(
        jnp.where(whole | rest, gate_ref[...].astype(jnp.float32), 0.0), axis=1, keepdims=True
    )
    rows = jnp.dot(
        whole.astype(jnp.bfloat16), part_ref[...], preferred_element_type=jnp.float32
    ) + jnp.dot(rest.astype(jnp.bfloat16), last_ref[...], preferred_element_type=jnp.float32)
    out = (rows * gate).astype(jnp.bfloat16)
    send_ref[...] = out.reshape(send_ref.shape)


def place(ids, gates, cotangent, experts):
    tokens, width = cotangent.shape
    quarter = width // ROWS
    return pl.pallas_call(
        lambda *refs: place_kernel(experts, *refs),
        grid=(CAP,),
        in_specs=[
            pl.BlockSpec((1, tokens), lambda c: (0, 0)),
            pl.BlockSpec((1, tokens), lambda c: (0, 0)),
            pl.BlockSpec((tokens, quarter), lambda c: (0, c)),
            pl.BlockSpec((tokens, quarter), lambda c: (0, CAP)),
        ],
        out_specs=[
            pl.BlockSpec((experts, ROWS, quarter), lambda c: (0, 0, c)),
            pl.BlockSpec((1, tokens), lambda c: (0, 0)),
        ],
        out_shape=[
            jax.ShapeDtypeStruct((experts, ROWS, CAP * quarter), jnp.bfloat16),
            jax.ShapeDtypeStruct((1, tokens), jnp.int32),
        ],
        name="place_rows",
    )(ids, gates, cotangent, cotangent)


def grads_kernel(got_ref, b_ref, low_ref, rest_ref, back_ref, hidden_ref, out_ref, gl_ref, sg_ref):
    slots, rank = low_ref.shape
    quarter = b_ref.shape[1] // ROWS
    across = (((1,), (1,)), ((), ()))
    down = (((0,), (0,)), ((), ()))
    place_in = lax.broadcasted_iota(jnp.int32, (slots, rank), 0) % ROWS
    low = low_ref[...]
    total = jnp.zeros((slots, rank), jnp.float32)
    last = jnp.zeros((quarter, rank), jnp.float32)
    cut = out_ref.shape[0]
    a_rows = hidden_ref.shape[1] // cut
    b_rows = b_ref.shape[1] // cut
    per = cut // ROWS
    for c in range(CAP):
        x = got_ref[:, :, c * quarter : (c + 1) * quarter].reshape(slots, quarter)
        main = lax.dot_general(
            x, b_ref[:, c * quarter : (c + 1) * quarter], across, preferred_element_type=jnp.float32
        )
        rest = lax.dot_general(
            x, b_ref[:, CAP * quarter :], across, preferred_element_type=jnp.float32
        )
        total = total + jnp.where(place_in < CAP, main, 0.0)
        rest = jnp.concatenate([rest[CAP - c :], rest[: CAP - c]], axis=0)
        total = total + jnp.where(place_in == c, rest, 0.0)
        both = lax.dot_general(
            x,
            jnp.concatenate([low, rest_ref[c]], axis=1),
            down,
            preferred_element_type=jnp.float32,
        )
        last = last + both[:, rank:]
        out_ref[c * per : (c + 1) * per, a_rows:, :] = (
            both[:, :rank].astype(jnp.bfloat16).reshape(per, b_rows, rank)
        )
    out_ref[CAP * per :, a_rows:, :] = last.astype(jnp.bfloat16).reshape(per, b_rows, rank)
    sg = jnp.sum(total * low.astype(jnp.float32), axis=1, keepdims=True)
    sg_ref[...] = jnp.broadcast_to(sg, (slots, rank))
    grad_low = jnp.dot(
        back_ref[...], total.astype(jnp.bfloat16), preferred_element_type=jnp.float32
    ).astype(jnp.bfloat16)
    gl_ref[...] = grad_low
    out_ref[:, :a_rows, :] = (
        lax.dot_general(hidden_ref[...], grad_low, down, preferred_element_type=jnp.float32)
        .astype(jnp.bfloat16)
        .reshape(cut, a_rows, rank)
    )


def slot_grads(got, b, low, rest, back, hidden, cut):
    slots, rank = low.shape
    rows = (hidden.shape[1] + b.shape[1]) // cut
    return pl.pallas_call(
        grads_kernel,
        out_shape=[
            jax.ShapeDtypeStruct((cut, rows, rank), jnp.bfloat16),
            jax.ShapeDtypeStruct((hidden.shape[0], rank), jnp.bfloat16),
            jax.ShapeDtypeStruct((slots, rank), jnp.float32),
        ],
        compiler_params=pltpu.CompilerParams(vmem_limit_bytes=48 * 2**20),
        name="slot_grads",
    )(got, b, low, rest, back, hidden)


def body(cotangent, gates, expert_ids, hidden, factor_a, factor_b):
    tokens = cotangent.shape[0]
    sources = lax.axis_size("expert")
    experts = 2 * sources
    groups = 2 * lax.axis_size("q")
    core = lax.axis_index("k")
    me = core * sources + lax.axis_index("expert")
    units, rank = factor_a.shape[1], factor_a.shape[2]
    width = factor_b.shape[2]
    a_rows = units // groups
    pair = [(0, 1), (1, 0)]

    send, row = place(expert_ids.reshape(1, tokens), gates.reshape(1, tokens), cotangent, experts)
    got = lax.all_to_all(send, SIDES, split_axis=0, concat_axis=0, tiled=True)

    saved = jnp.transpose(hidden[0], (0, 2, 1, 3)).reshape(2, CAP * sources, units)
    own = lax.dynamic_index_in_dim(saved, core, 0, keepdims=False)
    other = lax.ppermute(
        lax.dynamic_index_in_dim(saved, 1 - core, 0, keepdims=False), "k", pair
    )
    mine = jnp.where(core == 0, jnp.stack([own, other]), jnp.stack([other, own]))
    a_mine = lax.dynamic_index_in_dim(factor_a, core, 0, keepdims=False)
    b_mine = lax.dynamic_index_in_dim(factor_b, core, 0, keepdims=False)
    low = jnp.einsum("gsf,fr->gsr", mine, a_mine, preferred_element_type=jnp.float32).astype(
        jnp.bfloat16
    )
    low = low.reshape(2, CAP, sources, rank)
    by_source = jnp.transpose(low, (0, 2, 1, 3)).reshape(experts, CAP, rank)
    whole = jnp.pad(by_source, ((0, 0), (0, 1), (0, 0))).reshape(experts * ROWS, rank)
    rest = jnp.pad(
        jnp.transpose(by_source, (1, 0, 2))[:, :, None, :], ((0, 0), (0, 0), (CAP, 0), (0, 0))
    ).reshape(CAP, experts * ROWS, rank)
    slot = jnp.arange(experts * CAP, dtype=jnp.int32)
    group, place_c, source = slot // (CAP * sources), slot // sources % CAP, slot % sources
    at_row = (group * sources + source) * ROWS + place_c
    back_rows = (
        at_row[:, None] == jnp.arange(experts * ROWS, dtype=jnp.int32)[None, :]
    ).astype(jnp.bfloat16)

    parts, grad_low, slot_gate = slot_grads(
        got, b_mine, whole, rest, back_rows, mine.reshape(2 * CAP * sources, units), groups
    )
    summed = lax.all_to_all(parts, GROUPS, split_axis=0, concat_axis=0, tiled=True)
    summed = jnp.sum(
        summed.reshape(groups // 2, 2, *summed.shape[1:]).astype(jnp.float32), axis=0
    )
    grad_a = summed[:, :a_rows]
    grad_b = jnp.transpose(summed[:, a_rows:], (0, 2, 1))

    grad_low = grad_low.reshape(2, CAP * sources, rank)
    kept = lax.dynamic_index_in_dim(grad_low, core, 0, keepdims=False)
    sent = lax.ppermute(
        lax.dynamic_index_in_dim(grad_low, 1 - core, 0, keepdims=False), "k", pair
    )
    grad_low = jnp.where(core == 0, jnp.stack([kept, sent]), jnp.stack([sent, kept]))
    grad_hidden = jnp.einsum(
        "lsr,lfr->lsf", grad_low, factor_a, preferred_element_type=jnp.float32
    ).astype(jnp.bfloat16)
    grad_hidden = jnp.transpose(grad_hidden.reshape(2, CAP, sources, units), (0, 2, 1, 3))

    slot_gate = slot_gate[:, 0].reshape(experts, ROWS)
    away = jnp.arange(experts, dtype=jnp.int32) ^ me
    pick = (away[:, None] == jnp.arange(experts, dtype=jnp.int32)[None, :]).astype(jnp.float32)
    home = jnp.dot(pick, slot_gate, precision=lax.Precision.HIGHEST)
    bit = 1
    while bit < experts:
        home = home.reshape(experts // (2 * bit), 2, bit, ROWS)
        if bit < sources:
            there = [(i, i ^ bit) for i in range(sources)]
            moved = lax.ppermute(home[:, 1], "expert", there)
        else:
            moved = lax.ppermute(home[:, 1], "k", pair)
        home = jnp.stack([home[:, 0], moved], axis=1)
        bit *= 2
    row = row.reshape(tokens)
    row = ((row // ROWS) ^ me) * ROWS + row % ROWS
    chosen = (row[:, None] == jnp.arange(experts * ROWS, dtype=jnp.int32)[None, :]).astype(
        jnp.float32
    )
    grad_gates = jnp.dot(
        chosen, home.reshape(experts * ROWS, 1), precision=lax.Precision.HIGHEST
    ) / gates.astype(jnp.float32)
    return grad_a, grad_b, grad_hidden[None], grad_gates


def solution(mesh):
    fine = Mesh(
        mesh.devices.reshape(mesh.shape["dp"] // 2, 2, mesh.shape["expert"]),
        ("q", "k", "expert"),
    )
    dp = GROUPS
    tokens = P(("q", "k", "expert"), None)
    return jax.shard_map(
        body,
        mesh=fine,
        in_specs=(
            tokens,
            tokens,
            tokens,
            P(dp, "expert", None, None, None),
            P("expert", None, None),
            P("expert", None, None),
        ),
        out_specs=(
            P("expert", dp, None),
            P("expert", None, dp),
            P(dp, "expert", None, None, None),
            tokens,
        ),
        check_vma=False,
    )
```

```python
import jax
import jax.numpy as jnp
from jax import lax
from jax.experimental import pallas as pl
from jax.experimental.pallas import tpu as pltpu
from jax.sharding import Mesh, PartitionSpec as P

CAP = 3
ROWS = 4
EXPERT = ("x", "z")
SIDES = ("k",) + EXPERT
GROUPS = ("q", "k")


def place_kernel(experts, ids_ref, gate_ref, part_ref, last_ref, send_ref, row_ref):
    tokens = ids_ref.shape[1]
    ids = ids_ref[...]
    expert = lax.broadcasted_iota(jnp.int32, (experts, tokens), 0)
    named = expert == ids
    older = lax.broadcasted_iota(jnp.int32, (tokens, tokens), 0)
    newer = lax.broadcasted_iota(jnp.int32, (tokens, tokens), 1)
    before = jnp.dot(
        named.astype(jnp.bfloat16),
        (older < newer).astype(jnp.bfloat16),
        preferred_element_type=jnp.float32,
    )
    rank = jnp.sum(jnp.where(named, before, 0.0), axis=0, keepdims=True).astype(jnp.int32)
    block = (ids % 2) * (experts // 2) + ids // 2
    row_ref[...] = rank

    c = pl.program_id(0)
    row = lax.broadcasted_iota(jnp.int32, (experts * ROWS, tokens), 0)
    whole = row == block * ROWS + rank
    rest = (row == block * ROWS + CAP) & (rank == c)
    gate = jnp.sum(
        jnp.where(whole | rest, gate_ref[...].astype(jnp.float32), 0.0), axis=1, keepdims=True
    )
    rows = jnp.dot(
        jnp.concatenate([whole.astype(jnp.bfloat16), rest.astype(jnp.bfloat16)], axis=1),
        jnp.concatenate([part_ref[...], last_ref[...]], axis=0),
        preferred_element_type=jnp.float32,
    )
    out = (rows * gate).astype(jnp.bfloat16)
    send_ref[...] = out.reshape(send_ref.shape)


def place(ids, gates, cotangent, experts):
    tokens, width = cotangent.shape
    quarter = width // ROWS
    return pl.pallas_call(
        lambda *refs: place_kernel(experts, *refs),
        grid=(CAP,),
        in_specs=[
            pl.BlockSpec((1, tokens), lambda c: (0, 0)),
            pl.BlockSpec((1, tokens), lambda c: (0, 0)),
            pl.BlockSpec((tokens, quarter), lambda c: (0, c)),
            pl.BlockSpec((tokens, quarter), lambda c: (0, CAP)),
        ],
        out_specs=[
            pl.BlockSpec((experts, ROWS, quarter), lambda c: (0, 0, c)),
            pl.BlockSpec((1, tokens), lambda c: (0, 0)),
        ],
        out_shape=[
            jax.ShapeDtypeStruct((experts, ROWS, CAP * quarter), jnp.bfloat16),
            jax.ShapeDtypeStruct((1, tokens), jnp.int32),
        ],
        name="place_rows",
    )(ids, gates, cotangent, cotangent)


def grads_kernel(
    got_hbm, b_ref, low_ref, rest_ref, back_ref, hidden_ref, out_hbm, gl_ref, sg_ref,
    got, out, got_sem, out_sem,
):
    slots, rank = low_ref.shape
    quarter = b_ref.shape[1] // ROWS
    across = (((1,), (1,)), ((), ()))
    down = (((0,), (0,)), ((), ()))
    cut = out_hbm.shape[0]
    a_rows = hidden_ref.shape[1] // cut
    b_rows = b_ref.shape[1] // cut
    per = cut // ROWS

    def fetch(c):
        columns = pl.ds(c * quarter, quarter)
        return pltpu.make_async_copy(
            got_hbm.at[:, :, columns], got.at[:, :, columns], got_sem.at[c]
        )

    def store(c):
        part = (pl.ds(c * per, per), pl.ds(a_rows, b_rows))
        return pltpu.make_async_copy(out.at[part], out_hbm.at[part], out_sem.at[c])

    for c in range(CAP):
        fetch(c).start()
    place_in = lax.broadcasted_iota(jnp.int32, (slots, rank), 0) % ROWS
    low = low_ref[...]
    total = jnp.zeros((slots, rank), jnp.float32)
    last = jnp.zeros((quarter, rank), jnp.float32)
    for c in range(CAP):
        fetch(c).wait()
        x = got[:, :, c * quarter : (c + 1) * quarter].reshape(slots, quarter)
        main = lax.dot_general(
            x, b_ref[:, c * quarter : (c + 1) * quarter], across, preferred_element_type=jnp.float32
        )
        rest = lax.dot_general(
            x, b_ref[:, CAP * quarter :], across, preferred_element_type=jnp.float32
        )
        total = total + jnp.where(place_in < CAP, main, 0.0)
        rest = jnp.concatenate([rest[CAP - c :], rest[: CAP - c]], axis=0)
        total = total + jnp.where(place_in == c, rest, 0.0)
        both = lax.dot_general(
            x,
            jnp.concatenate([low, rest_ref[c]], axis=1),
            down,
            preferred_element_type=jnp.float32,
        )
        last = last + both[:, rank:]
        out[c * per : (c + 1) * per, a_rows:, :] = (
            both[:, :rank].astype(jnp.bfloat16).reshape(per, b_rows, rank)
        )
        store(c).start()
    out[CAP * per :, a_rows:, :] = last.astype(jnp.bfloat16).reshape(per, b_rows, rank)
    store(CAP).start()

    sg_ref[...] = lax.dot_general(
        jnp.ones((sg_ref.shape[0], rank), jnp.float32),
        total * low.astype(jnp.float32),
        across,
        precision=lax.Precision.HIGHEST,
        preferred_element_type=jnp.float32,
    )
    moved = jnp.dot(
        back_ref[...], total.astype(jnp.bfloat16), preferred_element_type=jnp.float32
    ).astype(jnp.bfloat16)
    gl_ref[...] = moved
    out[:, :a_rows, :] = (
        lax.dot_general(hidden_ref[...], moved, down, preferred_element_type=jnp.float32)
        .astype(jnp.bfloat16)
        .reshape(cut, a_rows, rank)
    )
    first = (slice(None), pl.ds(0, a_rows))
    copy = pltpu.make_async_copy(out.at[first], out_hbm.at[first], out_sem.at[ROWS])
    copy.start()
    for c in range(ROWS):
        store(c).wait()
    copy.wait()


def slot_grads(got, b, low, rest, back, hidden, cut):
    slots, rank = low.shape
    rows = (hidden.shape[1] + b.shape[1]) // cut
    whole = pl.BlockSpec(memory_space=pltpu.VMEM)
    return pl.pallas_call(
        grads_kernel,
        in_specs=[pl.BlockSpec(memory_space=pltpu.HBM)] + [whole] * 5,
        out_specs=[pl.BlockSpec(memory_space=pltpu.HBM), whole, whole],
        out_shape=[
            jax.ShapeDtypeStruct((cut, rows, rank), jnp.bfloat16),
            jax.ShapeDtypeStruct((hidden.shape[0], rank), jnp.bfloat16),
            jax.ShapeDtypeStruct((8, slots), jnp.float32),
        ],
        scratch_shapes=[
            pltpu.VMEM(got.shape, jnp.bfloat16),
            pltpu.VMEM((cut, rows, rank), jnp.bfloat16),
            pltpu.SemaphoreType.DMA((CAP,)),
            pltpu.SemaphoreType.DMA((ROWS + 1,)),
        ],
        compiler_params=pltpu.CompilerParams(vmem_limit_bytes=48 * 2**20),
        name="slot_grads",
    )(got, b, low, rest, back, hidden)


def add_kernel(parts_ref, a_ref, b_ref):
    total = jnp.sum(parts_ref[...].astype(jnp.float32), axis=0)
    a_rows = a_ref.shape[1]
    a_ref[...] = total[:, :a_rows]
    b_ref[...] = total[:, a_rows:]


def add_parts(parts, a_rows):
    count, rows, rank = parts.shape
    b_rows = rows - a_rows
    return pl.pallas_call(
        add_kernel,
        grid=(2,),
        in_specs=[pl.BlockSpec((count // 2, 1, rows, rank), lambda i: (0, i, 0, 0))],
        out_specs=[
            pl.BlockSpec((1, a_rows, rank), lambda i: (i, 0, 0)),
            pl.BlockSpec((1, b_rows, rank), lambda i: (i, 0, 0)),
        ],
        out_shape=[
            jax.ShapeDtypeStruct((2, a_rows, rank), jnp.float32),
            jax.ShapeDtypeStruct((2, b_rows, rank), jnp.float32),
        ],
        name="add_parts",
    )(parts.reshape(count // 2, 2, rows, rank))


def body(cotangent, gates, expert_ids, hidden, factor_a, factor_b):
    tokens = cotangent.shape[0]
    sources = lax.axis_size("x") * lax.axis_size("z")
    experts = 2 * sources
    groups = 2 * lax.axis_size("q")
    core = lax.axis_index("k")
    units, rank = factor_a.shape[1], factor_a.shape[2]
    width = factor_b.shape[2]
    a_rows = units // groups
    pair = [(0, 1), (1, 0)]

    send, row = place(expert_ids.reshape(1, tokens), gates.reshape(1, tokens), cotangent, experts)
    got = lax.all_to_all(send, SIDES, split_axis=0, concat_axis=0, tiled=True)

    saved = jnp.transpose(hidden[0], (0, 2, 1, 3)).reshape(2, CAP * sources, units)
    own = lax.dynamic_index_in_dim(saved, core, 0, keepdims=False)
    other = lax.ppermute(
        lax.dynamic_index_in_dim(saved, 1 - core, 0, keepdims=False), "k", pair
    )
    mine = jnp.where(core == 0, jnp.stack([own, other]), jnp.stack([other, own]))
    a_mine = lax.dynamic_index_in_dim(factor_a, core, 0, keepdims=False)
    b_mine = lax.dynamic_index_in_dim(factor_b, core, 0, keepdims=False)
    low = jnp.einsum("gsf,fr->gsr", mine, a_mine, preferred_element_type=jnp.float32).astype(
        jnp.bfloat16
    )
    low = low.reshape(2, CAP, sources, rank)
    by_source = jnp.transpose(low, (0, 2, 1, 3)).reshape(experts, CAP, rank)
    whole = jnp.pad(by_source, ((0, 0), (0, 1), (0, 0))).reshape(experts * ROWS, rank)
    rest = jnp.pad(
        jnp.transpose(by_source, (1, 0, 2))[:, :, None, :], ((0, 0), (0, 0), (CAP, 0), (0, 0))
    ).reshape(CAP, experts * ROWS, rank)
    slot = jnp.arange(experts * CAP, dtype=jnp.int32)
    group, place_c, source = slot // (CAP * sources), slot // sources % CAP, slot % sources
    at_row = (group * sources + source) * ROWS + place_c
    back_rows = (
        at_row[:, None] == jnp.arange(experts * ROWS, dtype=jnp.int32)[None, :]
    ).astype(jnp.bfloat16)

    parts, grad_low, slot_gate = slot_grads(
        got, b_mine, whole, rest, back_rows, mine.reshape(2 * CAP * sources, units), groups
    )

    line = lax.axis_size("z")
    along = lax.all_gather(slot_gate, "z", axis=0, tiled=True)
    along = along.reshape(line, slot_gate.shape[0], experts * ROWS)[:, 0]

    summed = lax.all_to_all(parts, GROUPS, split_axis=0, concat_axis=0, tiled=True)
    grad_a, grad_b = add_parts(summed, a_rows)
    grad_b = jnp.transpose(grad_b, (0, 2, 1))

    corner = core * lax.axis_size("x") + lax.axis_index("x")
    corners = 2 * lax.axis_size("x")
    target = (jnp.arange(corners, dtype=jnp.int32) ^ corner) * line + lax.axis_index("z")
    columns = target[:, None] * ROWS + jnp.arange(ROWS, dtype=jnp.int32)[None, :]
    pick = (
        jnp.arange(experts * ROWS, dtype=jnp.int32)[:, None, None] == columns[None]
    ).astype(jnp.float32)
    home = jnp.einsum("zs,sdr->dzr", along, pick, precision=lax.Precision.HIGHEST)
    pieces = [home[0]]
    for d in range(1, corners):
        there = [(i, i ^ d) for i in range(corners)]
        pieces.append(lax.ppermute(home[d], ("k", "x"), there))
    home = jnp.stack(pieces)
    ids = expert_ids.reshape(tokens)
    owner = ids // 2
    entry = (((ids % 2) * lax.axis_size("x") + owner // line) ^ corner) * line + owner % line
    entry = entry * ROWS + row.reshape(tokens)
    chosen = (
        entry[:, None] == jnp.arange(experts * ROWS, dtype=jnp.int32)[None, :]
    ).astype(jnp.float32)
    grad_gates = jnp.dot(
        chosen, home.reshape(experts * ROWS, 1), precision=lax.Precision.HIGHEST
    ) / gates.astype(jnp.float32)

    grad_low = grad_low.reshape(2, CAP * sources, rank)
    kept = lax.dynamic_index_in_dim(grad_low, core, 0, keepdims=False)
    sent = lax.ppermute(
        lax.dynamic_index_in_dim(grad_low, 1 - core, 0, keepdims=False), "k", pair
    )
    grad_low = jnp.where(core == 0, jnp.stack([kept, sent]), jnp.stack([sent, kept]))
    grad_hidden = jnp.einsum(
        "lsr,lfr->lsf", grad_low, factor_a, preferred_element_type=jnp.float32
    ).astype(jnp.bfloat16)
    grad_hidden = jnp.transpose(grad_hidden.reshape(2, CAP, sources, units), (0, 2, 1, 3))
    return grad_a, grad_b, grad_hidden[None], grad_gates


def solution(mesh):
    groups, sources = mesh.shape["dp"], mesh.shape["expert"]
    fine = Mesh(
        mesh.devices.reshape(groups // 2, 2, 2, sources // 2), ("q", "k", "x", "z")
    )
    dp = GROUPS
    tokens = P(("q", "k", "x", "z"), None)
    return jax.shard_map(
        body,
        mesh=fine,
        in_specs=(
            tokens,
            tokens,
            tokens,
            P(dp, EXPERT, None, None, None),
            P(EXPERT, None, None),
            P(EXPERT, None, None),
        ),
        out_specs=(
            P(EXPERT, dp, None),
            P(EXPERT, None, dp),
            P(dp, EXPERT, None, None, None),
            tokens,
        ),
        check_vma=False,
    )
```

```python
import jax
import jax.numpy as jnp
from jax import lax
from jax.experimental import pallas as pl
from jax.experimental.pallas import tpu as pltpu
from jax.sharding import Mesh, PartitionSpec as P

CAP = 3
ROWS = 4
RIDE = 16
VMEM = 60 * 2**20
EXPERT = ("x", "z")
SIDES = ("k",) + EXPERT
GROUPS = ("q", "k")


def place_kernel(ids_ref, gate_ref, dy_hbm, send_hbm, row_ref, dy, send, in_sem, out_sem):
    experts = send_hbm.shape[0]
    tokens, width = dy.shape
    quarter = width // ROWS

    def fetch(c):
        part = (slice(None), pl.ds(c * quarter, quarter))
        return pltpu.make_async_copy(dy_hbm.at[part], dy.at[part], in_sem.at[c])

    def store(c):
        part = (slice(None), slice(None), pl.ds(c * quarter, quarter))
        return pltpu.make_async_copy(send.at[part], send_hbm.at[part], out_sem.at[c])

    for c in (CAP, *range(CAP)):
        fetch(c).start()
    ids = ids_ref[...]
    expert = lax.broadcasted_iota(jnp.int32, (experts, tokens), 0)
    named = expert == ids
    older = lax.broadcasted_iota(jnp.int32, (tokens, tokens), 0)
    newer = lax.broadcasted_iota(jnp.int32, (tokens, tokens), 1)
    before = jnp.dot(
        named.astype(jnp.bfloat16),
        (older < newer).astype(jnp.bfloat16),
        preferred_element_type=jnp.float32,
    )
    rank = jnp.sum(jnp.where(named, before, 0.0), axis=0, keepdims=True).astype(jnp.int32)
    row_ref[...] = rank
    block = (ids % 2) * (experts // 2) + ids // 2
    row = lax.broadcasted_iota(jnp.int32, (experts * ROWS, tokens), 0)
    whole = row == block * ROWS + rank
    last = row == block * ROWS + CAP
    gates = jnp.broadcast_to(gate_ref[...].astype(jnp.float32), whole.shape)
    fetch(CAP).wait()
    for c in range(CAP):
        rest = last & (rank == c)
        gate = jnp.sum(jnp.where(whole | rest, gates, 0.0), axis=1, keepdims=True)
        pick = jnp.concatenate([whole.astype(jnp.bfloat16), rest.astype(jnp.bfloat16)], axis=1)
        fetch(c).wait()
        columns = slice(c * quarter, (c + 1) * quarter)
        rows = jnp.dot(
            pick,
            jnp.concatenate([dy[:, columns], dy[:, CAP * quarter :]], axis=0),
            preferred_element_type=jnp.float32,
        )
        send[:, :, columns] = (rows * gate).astype(jnp.bfloat16).reshape(experts, ROWS, quarter)
        store(c).start()
    for c in range(CAP):
        store(c).wait()


def place(ids, gates, cotangent, experts):
    tokens, width = cotangent.shape
    shape = (experts, ROWS, CAP * (width // ROWS))
    whole = pl.BlockSpec(memory_space=pltpu.VMEM)
    return pl.pallas_call(
        place_kernel,
        in_specs=[whole, whole, pl.BlockSpec(memory_space=pl.ANY)],
        out_specs=[pl.BlockSpec(memory_space=pl.ANY), whole],
        out_shape=[
            jax.ShapeDtypeStruct(shape, jnp.bfloat16),
            jax.ShapeDtypeStruct((1, tokens), jnp.int32),
        ],
        scratch_shapes=[
            pltpu.VMEM((tokens, width), jnp.bfloat16),
            pltpu.VMEM(shape, jnp.bfloat16),
            pltpu.SemaphoreType.DMA((ROWS,)),
            pltpu.SemaphoreType.DMA((CAP,)),
        ],
        compiler_params=pltpu.CompilerParams(vmem_limit_bytes=VMEM),
        name="place_rows",
    )(ids, gates, cotangent)


def grads_kernel(
    core_ref, got_hbm, b_ref, low_ref, rest_ref, back_ref, hidden, out, gl_ref, got, got_sem
):
    slots, rank = low_ref.shape
    core, width = core_ref[0], b_ref.shape[2]
    quarter = width // ROWS
    across = (((1,), (1,)), ((), ()))
    down = (((0,), (0,)), ((), ()))
    cut = out.shape[0]
    a_rows = hidden.shape[1] // cut
    b_rows = width // cut
    per = cut // ROWS

    def fetch(c):
        columns = pl.ds(c * quarter, quarter)
        return pltpu.make_async_copy(
            got_hbm.at[:, :, columns], got.at[:, :, columns], got_sem.at[c]
        )

    for c in range(CAP):
        fetch(c).start()
    place_in = lax.broadcasted_iota(jnp.int32, (slots, rank), 0) % ROWS
    low = low_ref[...]
    total = jnp.zeros((slots, rank), jnp.float32)
    last = jnp.zeros((quarter, rank), jnp.float32)
    for c in range(CAP):
        fetch(c).wait()
        x = got[:, :, c * quarter : (c + 1) * quarter].reshape(slots, quarter)
        main = lax.dot_general(
            x,
            b_ref[core, :, c * quarter : (c + 1) * quarter],
            across,
            preferred_element_type=jnp.float32,
        )
        rest = lax.dot_general(
            x, b_ref[core, :, CAP * quarter :], across, preferred_element_type=jnp.float32
        )
        total = total + jnp.where(place_in < CAP, main, 0.0)
        rest = jnp.concatenate([rest[CAP - c :], rest[: CAP - c]], axis=0)
        total = total + jnp.where(place_in == c, rest, 0.0)
        both = lax.dot_general(
            x,
            jnp.concatenate([low, rest_ref[c]], axis=1),
            down,
            preferred_element_type=jnp.float32,
        )
        last = last + both[:, rank:]
        out[c * per : (c + 1) * per, a_rows:, :] = (
            both[:, :rank].astype(jnp.bfloat16).reshape(per, b_rows, rank)
        )
    out[CAP * per :, a_rows:, :] = last.astype(jnp.bfloat16).reshape(per, b_rows, rank)

    grad_low = jnp.dot(
        back_ref[...], total.astype(jnp.bfloat16), preferred_element_type=jnp.float32
    ).astype(jnp.bfloat16)
    out[:, :a_rows, :] = (
        lax.dot_general(hidden[...], grad_low, down, preferred_element_type=jnp.float32)
        .astype(jnp.bfloat16)
        .reshape(cut, a_rows, rank)
    )
    sg = lax.dot_general(
        jnp.ones((RIDE, rank), jnp.float32),
        total * low.astype(jnp.float32),
        across,
        precision=lax.Precision.HIGHEST,
        preferred_element_type=jnp.float32,
    )
    head = sg.astype(jnp.bfloat16).astype(jnp.float32)
    line = lax.broadcasted_iota(jnp.int32, sg.shape, 0)
    ride = jnp.where(line == 0, head, jnp.where(line == 1, sg - head, 0.0)).astype(jnp.bfloat16)
    count = grad_low.shape[0] // 2
    for group in range(2):
        gl_ref[group, :count] = grad_low[group * count : (group + 1) * count]
        gl_ref[group, count:] = ride[:, group * (slots // 2) : (group + 1) * (slots // 2)]


def slot_grads(core, got, b, low, rest, back, hidden, cut):
    slots, rank = low.shape
    rows = (hidden.shape[1] + b.shape[2]) // cut
    whole = pl.BlockSpec(memory_space=pltpu.VMEM)
    return pl.pallas_call(
        grads_kernel,
        in_specs=[pl.BlockSpec(memory_space=pltpu.SMEM), pl.BlockSpec(memory_space=pl.ANY)]
        + [whole] * 5,
        out_specs=[whole, whole],
        out_shape=[
            jax.ShapeDtypeStruct((cut, rows, rank), jnp.bfloat16),
            jax.ShapeDtypeStruct((2, hidden.shape[0] // 2 + RIDE, rank), jnp.bfloat16),
        ],
        scratch_shapes=[
            pltpu.VMEM(got.shape, jnp.bfloat16),
            pltpu.SemaphoreType.DMA((CAP,)),
        ],
        compiler_params=pltpu.CompilerParams(vmem_limit_bytes=48 * 2**20),
        name="slot_grads",
    )(core.reshape(1), got, b, low, rest, back, hidden)


def add_kernel(parts_ref, a_ref, b_ref):
    total = jnp.sum(parts_ref[...].astype(jnp.float32), axis=0)
    a_rows = a_ref.shape[1]
    a_ref[...] = total[:, :a_rows]
    b_ref[...] = total[:, a_rows:]


def add_parts(parts, a_rows):
    count, rows, rank = parts.shape
    b_rows = rows - a_rows
    return pl.pallas_call(
        add_kernel,
        grid=(2,),
        in_specs=[pl.BlockSpec((count // 2, 1, rows, rank), lambda i: (0, i, 0, 0))],
        out_specs=[
            pl.BlockSpec((1, a_rows, rank), lambda i: (i, 0, 0)),
            pl.BlockSpec((1, b_rows, rank), lambda i: (i, 0, 0)),
        ],
        out_shape=[
            jax.ShapeDtypeStruct((2, a_rows, rank), jnp.float32),
            jax.ShapeDtypeStruct((2, b_rows, rank), jnp.float32),
        ],
        compiler_params=pltpu.CompilerParams(vmem_limit_bytes=63 * 2**20),
        name="add_parts",
    )(parts.reshape(count // 2, 2, rows, rank))


def body(cotangent, gates, expert_ids, hidden, factor_a, factor_b):
    tokens = cotangent.shape[0]
    sources = lax.axis_size("x") * lax.axis_size("z")
    experts = 2 * sources
    groups = 2 * lax.axis_size("q")
    core = lax.axis_index("k")
    units, rank = factor_a.shape[1], factor_a.shape[2]
    width = factor_b.shape[2]
    a_rows = units // groups
    pair = [(0, 1), (1, 0)]

    send, row = place(expert_ids.reshape(1, tokens), gates.reshape(1, tokens), cotangent, experts)
    got = lax.all_to_all(send, SIDES, split_axis=0, concat_axis=0, tiled=True)

    saved = jnp.transpose(hidden[0], (0, 2, 1, 3)).reshape(2, CAP * sources, units)
    own = lax.dynamic_index_in_dim(saved, core, 0, keepdims=False)
    other = lax.ppermute(
        lax.dynamic_index_in_dim(saved, 1 - core, 0, keepdims=False), "k", pair
    )
    mine = jnp.where(core == 0, jnp.stack([own, other]), jnp.stack([other, own]))
    a_mine = lax.dynamic_index_in_dim(factor_a, core, 0, keepdims=False)
    low = jnp.einsum("gsf,fr->gsr", mine, a_mine, preferred_element_type=jnp.float32).astype(
        jnp.bfloat16
    )
    low = low.reshape(2, CAP, sources, rank)
    by_source = jnp.transpose(low, (0, 2, 1, 3)).reshape(experts, CAP, rank)
    whole = jnp.pad(by_source, ((0, 0), (0, 1), (0, 0))).reshape(experts * ROWS, rank)
    rest = jnp.pad(
        jnp.transpose(by_source, (1, 0, 2))[:, :, None, :], ((0, 0), (0, 0), (CAP, 0), (0, 0))
    ).reshape(CAP, experts * ROWS, rank)
    slot = jnp.arange(experts * CAP, dtype=jnp.int32)
    group, place_c, source = slot // (CAP * sources), slot // sources % CAP, slot % sources
    at_row = (group * sources + source) * ROWS + place_c
    back_rows = (
        at_row[:, None] == jnp.arange(experts * ROWS, dtype=jnp.int32)[None, :]
    ).astype(jnp.bfloat16)

    parts, grad_low = slot_grads(
        core, got, factor_b, whole, rest, back_rows, mine.reshape(2 * CAP * sources, units), groups
    )
    summed = lax.all_to_all(parts, GROUPS, split_axis=0, concat_axis=0, tiled=True)
    grad_a, grad_b = add_parts(summed, a_rows)
    grad_b = jnp.transpose(grad_b, (0, 2, 1))

    kept = lax.dynamic_index_in_dim(grad_low, core, 0, keepdims=False)
    sent = lax.ppermute(
        lax.dynamic_index_in_dim(grad_low, 1 - core, 0, keepdims=False), "k", pair
    )
    count = CAP * sources
    line, side = lax.axis_size("z"), lax.axis_index("x")
    riding = jnp.concatenate([kept[count : count + 2], sent[count : count + 2]])
    along = lax.all_gather(riding, "z", axis=0, tiled=True)
    along = jnp.sum(along.reshape(2 * line, 2, 2 * line * ROWS).astype(jnp.float32), axis=1)
    target = (jnp.arange(2, dtype=jnp.int32) ^ side) * line + lax.axis_index("z")
    columns = target[:, None] * ROWS + jnp.arange(ROWS, dtype=jnp.int32)[None, :]
    pick = (
        jnp.arange(2 * line * ROWS, dtype=jnp.int32)[:, None, None] == columns[None]
    ).astype(jnp.float32)
    home = jnp.einsum("zs,sdr->dzr", along, pick, precision=lax.Precision.HIGHEST)
    home = jnp.stack([home[0], lax.ppermute(home[1], "x", pair)])
    ids = expert_ids.reshape(tokens)
    owner = ids // 2
    entry = ((owner // line) ^ side) * line + owner % line
    entry = (entry * 2 + ((ids % 2) ^ core)) * ROWS + row.reshape(tokens)
    chosen = (
        entry[:, None] == jnp.arange(experts * ROWS, dtype=jnp.int32)[None, :]
    ).astype(jnp.float32)
    grad_gates = jnp.dot(
        chosen, home.reshape(experts * ROWS, 1), precision=lax.Precision.HIGHEST
    ) / gates.astype(jnp.float32)

    kept, sent = kept[:count], sent[:count]
    grad_low = jnp.where(core == 0, jnp.stack([kept, sent]), jnp.stack([sent, kept]))
    grad_hidden = jnp.einsum(
        "lsr,lfr->lsf", grad_low, factor_a, preferred_element_type=jnp.float32
    ).astype(jnp.bfloat16)
    grad_hidden = jnp.transpose(grad_hidden.reshape(2, CAP, sources, units), (0, 2, 1, 3))
    return grad_a, grad_b, grad_hidden[None], grad_gates


def solution(mesh):
    groups, sources = mesh.shape["dp"], mesh.shape["expert"]
    fine = Mesh(
        mesh.devices.reshape(groups // 2, 2, 2, sources // 2), ("q", "k", "x", "z")
    )
    dp = GROUPS
    tokens = P(("q", "k", "x", "z"), None)
    return jax.shard_map(
        body,
        mesh=fine,
        in_specs=(
            tokens,
            tokens,
            tokens,
            P(dp, EXPERT, None, None, None),
            P(EXPERT, None, None),
            P(EXPERT, None, None),
        ),
        out_specs=(
            P(EXPERT, dp, None),
            P(EXPERT, None, dp),
            P(dp, EXPERT, None, None, None),
            tokens,
        ),
        check_vma=False,
    )
```

```python
import jax
import jax.numpy as jnp
from jax import lax
from jax.experimental import pallas as pl
from jax.experimental.pallas import tpu as pltpu
from jax.sharding import Mesh, PartitionSpec as P

CAP = 3
ROWS = 4
RIDE = 16
EXPERT = ("x", "z")
SIDES = ("k",) + EXPERT
GROUPS = ("q", "k")


def place_kernel(ids_ref, gate_ref, dy_hbm, send_hbm, row_ref, dy, send, in_sem, out_sem):
    experts = send_hbm.shape[0]
    tokens, width = dy.shape
    quarter = width // ROWS

    def fetch(c):
        part = (slice(None), pl.ds(c * quarter, quarter))
        return pltpu.make_async_copy(dy_hbm.at[part], dy.at[part], in_sem.at[c])

    def store(c):
        part = (slice(None), slice(None), pl.ds(c * quarter, quarter))
        return pltpu.make_async_copy(send.at[part], send_hbm.at[part], out_sem.at[c])

    for c in (CAP, *range(CAP)):
        fetch(c).start()
    ids = ids_ref[...]
    expert = lax.broadcasted_iota(jnp.int32, (experts, tokens), 0)
    named = expert == ids
    older = lax.broadcasted_iota(jnp.int32, (tokens, tokens), 0)
    newer = lax.broadcasted_iota(jnp.int32, (tokens, tokens), 1)
    before = jnp.dot(
        named.astype(jnp.bfloat16),
        (older < newer).astype(jnp.bfloat16),
        preferred_element_type=jnp.float32,
    )
    rank = jnp.sum(jnp.where(named, before, 0.0), axis=0, keepdims=True).astype(jnp.int32)
    row_ref[...] = rank
    block = (ids % 2) * (experts // 2) + ids // 2
    row = lax.broadcasted_iota(jnp.int32, (experts * ROWS, tokens), 0)
    whole = row == block * ROWS + rank
    last = row == block * ROWS + CAP
    gates = jnp.broadcast_to(gate_ref[...].astype(jnp.float32), whole.shape)
    fetch(CAP).wait()
    for c in range(CAP):
        rest = last & (rank == c)
        gate = jnp.sum(jnp.where(whole | rest, gates, 0.0), axis=1, keepdims=True)
        pick = jnp.concatenate([whole.astype(jnp.bfloat16), rest.astype(jnp.bfloat16)], axis=1)
        fetch(c).wait()
        columns = slice(c * quarter, (c + 1) * quarter)
        rows = jnp.dot(
            pick,
            jnp.concatenate([dy[:, columns], dy[:, CAP * quarter :]], axis=0),
            preferred_element_type=jnp.float32,
        )
        send[:, :, columns] = (rows * gate).astype(jnp.bfloat16).reshape(experts, ROWS, quarter)
        store(c).start()
    for c in range(CAP):
        store(c).wait()


def place(ids, gates, cotangent, experts):
    tokens, width = cotangent.shape
    shape = (experts, ROWS, CAP * (width // ROWS))
    whole = pl.BlockSpec(memory_space=pltpu.VMEM)
    return pl.pallas_call(
        place_kernel,
        in_specs=[whole, whole, pl.BlockSpec(memory_space=pl.ANY)],
        out_specs=[pl.BlockSpec(memory_space=pl.ANY), whole],
        out_shape=[
            jax.ShapeDtypeStruct(shape, jnp.bfloat16),
            jax.ShapeDtypeStruct((1, tokens), jnp.int32),
        ],
        scratch_shapes=[
            pltpu.VMEM((tokens, width), jnp.bfloat16),
            pltpu.VMEM(shape, jnp.bfloat16),
            pltpu.SemaphoreType.DMA((ROWS,)),
            pltpu.SemaphoreType.DMA((CAP,)),
        ],
        name="place_rows",
    )(ids, gates, cotangent)


def grads_kernel(
    core_ref, got_hbm, b_ref, low_ref, rest_ref, back_ref, hidden, out, gl_ref, got, got_sem
):
    slots, rank = low_ref.shape
    core, width = core_ref[0], b_ref.shape[2]
    quarter = width // ROWS
    across = (((1,), (1,)), ((), ()))
    down = (((0,), (0,)), ((), ()))
    cut = out.shape[0]
    a_rows = hidden.shape[1] // cut
    b_rows = width // cut
    per = cut // ROWS

    def fetch(c):
        columns = pl.ds(c * quarter, quarter)
        return pltpu.make_async_copy(
            got_hbm.at[:, :, columns], got.at[:, :, columns], got_sem.at[c]
        )

    for c in range(CAP):
        fetch(c).start()
    place_in = lax.broadcasted_iota(jnp.int32, (slots, rank), 0) % ROWS
    low = low_ref[...]
    total = jnp.zeros((slots, rank), jnp.float32)
    last = jnp.zeros((quarter, rank), jnp.float32)
    for c in range(CAP):
        fetch(c).wait()
        x = got[:, :, c * quarter : (c + 1) * quarter].reshape(slots, quarter)
        main = lax.dot_general(
            x,
            b_ref[core, :, c * quarter : (c + 1) * quarter],
            across,
            preferred_element_type=jnp.float32,
        )
        rest = lax.dot_general(
            x, b_ref[core, :, CAP * quarter :], across, preferred_element_type=jnp.float32
        )
        total = total + jnp.where(place_in < CAP, main, 0.0)
        rest = jnp.concatenate([rest[CAP - c :], rest[: CAP - c]], axis=0)
        total = total + jnp.where(place_in == c, rest, 0.0)
        both = lax.dot_general(
            x,
            jnp.concatenate([low, rest_ref[c]], axis=1),
            down,
            preferred_element_type=jnp.float32,
        )
        last = last + both[:, rank:]
        out[c * per : (c + 1) * per, a_rows:, :] = (
            both[:, :rank].astype(jnp.bfloat16).reshape(per, b_rows, rank)
        )
    out[CAP * per :, a_rows:, :] = last.astype(jnp.bfloat16).reshape(per, b_rows, rank)

    grad_low = jnp.dot(
        back_ref[...], total.astype(jnp.bfloat16), preferred_element_type=jnp.float32
    ).astype(jnp.bfloat16)
    out[:, :a_rows, :] = (
        lax.dot_general(hidden[...], grad_low, down, preferred_element_type=jnp.float32)
        .astype(jnp.bfloat16)
        .reshape(cut, a_rows, rank)
    )
    sg = lax.dot_general(
        jnp.ones((RIDE, rank), jnp.float32),
        total * low.astype(jnp.float32),
        across,
        precision=lax.Precision.HIGHEST,
        preferred_element_type=jnp.float32,
    )
    head = sg.astype(jnp.bfloat16).astype(jnp.float32)
    line = lax.broadcasted_iota(jnp.int32, sg.shape, 0)
    ride = jnp.where(line == 0, head, jnp.where(line == 1, sg - head, 0.0)).astype(jnp.bfloat16)
    count = grad_low.shape[0] // 2
    for group in range(2):
        gl_ref[group, :count] = grad_low[group * count : (group + 1) * count]
        gl_ref[group, count:] = ride[:, group * (slots // 2) : (group + 1) * (slots // 2)]


def slot_grads(core, got, b, low, rest, back, hidden, cut):
    slots, rank = low.shape
    rows = (hidden.shape[1] + b.shape[2]) // cut
    whole = pl.BlockSpec(memory_space=pltpu.VMEM)
    return pl.pallas_call(
        grads_kernel,
        in_specs=[pl.BlockSpec(memory_space=pltpu.SMEM), pl.BlockSpec(memory_space=pl.ANY)]
        + [whole] * 5,
        out_specs=[whole, whole],
        out_shape=[
            jax.ShapeDtypeStruct((cut, rows, rank), jnp.bfloat16),
            jax.ShapeDtypeStruct((2, hidden.shape[0] // 2 + RIDE, rank), jnp.bfloat16),
        ],
        scratch_shapes=[
            pltpu.VMEM(got.shape, jnp.bfloat16),
            pltpu.SemaphoreType.DMA((CAP,)),
        ],
        compiler_params=pltpu.CompilerParams(vmem_limit_bytes=24 * 2**20),
        name="slot_grads",
    )(core.reshape(1), got, b, low, rest, back, hidden)


def add_kernel(parts_ref, a_ref, b_ref):
    total = jnp.sum(parts_ref[...].astype(jnp.float32), axis=0)
    a_rows = a_ref.shape[1]
    a_ref[...] = total[:, :a_rows]
    b_ref[...] = total[:, a_rows:]


def add_parts(parts, a_rows):
    count, rows, rank = parts.shape
    b_rows = rows - a_rows
    return pl.pallas_call(
        add_kernel,
        grid=(2,),
        in_specs=[pl.BlockSpec((count // 2, 1, rows, rank), lambda i: (0, i, 0, 0))],
        out_specs=[
            pl.BlockSpec((1, a_rows, rank), lambda i: (i, 0, 0)),
            pl.BlockSpec((1, b_rows, rank), lambda i: (i, 0, 0)),
        ],
        out_shape=[
            jax.ShapeDtypeStruct((2, a_rows, rank), jnp.float32),
            jax.ShapeDtypeStruct((2, b_rows, rank), jnp.float32),
        ],
        compiler_params=pltpu.CompilerParams(vmem_limit_bytes=63 * 2**20),
        name="add_parts",
    )(parts.reshape(count // 2, 2, rows, rank))


def body(cotangent, gates, expert_ids, hidden, factor_a, factor_b):
    tokens = cotangent.shape[0]
    sources = lax.axis_size("x") * lax.axis_size("z")
    experts = 2 * sources
    groups = 2 * lax.axis_size("q")
    core = lax.axis_index("k")
    units, rank = factor_a.shape[1], factor_a.shape[2]
    width = factor_b.shape[2]
    a_rows = units // groups
    pair = [(0, 1), (1, 0)]

    send, row = place(expert_ids.reshape(1, tokens), gates.reshape(1, tokens), cotangent, experts)
    got = lax.all_to_all(send, SIDES, split_axis=0, concat_axis=0, tiled=True)

    saved = jnp.transpose(hidden[0], (0, 2, 1, 3)).reshape(2, CAP * sources, units)
    own = lax.dynamic_index_in_dim(saved, core, 0, keepdims=False)
    other = lax.ppermute(
        lax.dynamic_index_in_dim(saved, 1 - core, 0, keepdims=False), "k", pair
    )
    mine = jnp.where(core == 0, jnp.stack([own, other]), jnp.stack([other, own]))
    a_mine = lax.dynamic_index_in_dim(factor_a, core, 0, keepdims=False)
    low = jnp.einsum("gsf,fr->gsr", mine, a_mine, preferred_element_type=jnp.float32).astype(
        jnp.bfloat16
    )
    low = low.reshape(2, CAP, sources, rank)
    by_source = jnp.transpose(low, (0, 2, 1, 3)).reshape(experts, CAP, rank)
    whole = jnp.pad(by_source, ((0, 0), (0, 1), (0, 0))).reshape(experts * ROWS, rank)
    rest = jnp.pad(
        jnp.transpose(by_source, (1, 0, 2))[:, :, None, :], ((0, 0), (0, 0), (CAP, 0), (0, 0))
    ).reshape(CAP, experts * ROWS, rank)
    slot = jnp.arange(experts * CAP, dtype=jnp.int32)
    group, place_c, source = slot // (CAP * sources), slot // sources % CAP, slot % sources
    at_row = (group * sources + source) * ROWS + place_c
    back_rows = (
        at_row[:, None] == jnp.arange(experts * ROWS, dtype=jnp.int32)[None, :]
    ).astype(jnp.bfloat16)

    parts, grad_low = slot_grads(
        core, got, factor_b, whole, rest, back_rows, mine.reshape(2 * CAP * sources, units), groups
    )
    summed = lax.all_to_all(parts, GROUPS, split_axis=0, concat_axis=0, tiled=True)
    grad_a, grad_b = add_parts(summed, a_rows)
    grad_b = jnp.transpose(grad_b, (0, 2, 1))

    kept = lax.dynamic_index_in_dim(grad_low, core, 0, keepdims=False)
    sent = lax.ppermute(
        lax.dynamic_index_in_dim(grad_low, 1 - core, 0, keepdims=False), "k", pair
    )
    count = CAP * sources
    line, side = lax.axis_size("z"), lax.axis_index("x")
    riding = jnp.concatenate([kept[count : count + 2], sent[count : count + 2]])
    along = lax.all_gather(riding, "z", axis=0, tiled=True)
    along = jnp.sum(along.reshape(2 * line, 2, 2 * line * ROWS).astype(jnp.float32), axis=1)
    target = (jnp.arange(2, dtype=jnp.int32) ^ side) * line + lax.axis_index("z")
    columns = target[:, None] * ROWS + jnp.arange(ROWS, dtype=jnp.int32)[None, :]
    pick = (
        jnp.arange(2 * line * ROWS, dtype=jnp.int32)[:, None, None] == columns[None]
    ).astype(jnp.float32)
    home = jnp.einsum("zs,sdr->dzr", along, pick, precision=lax.Precision.HIGHEST)
    home = jnp.stack([home[0], lax.ppermute(home[1], "x", pair)])
    ids = expert_ids.reshape(tokens)
    owner = ids // 2
    entry = ((owner // line) ^ side) * line + owner % line
    entry = (entry * 2 + ((ids % 2) ^ core)) * ROWS + row.reshape(tokens)
    chosen = (
        entry[:, None] == jnp.arange(experts * ROWS, dtype=jnp.int32)[None, :]
    ).astype(jnp.float32)
    grad_gates = jnp.dot(
        chosen, home.reshape(experts * ROWS, 1), precision=lax.Precision.HIGHEST
    ) / gates.astype(jnp.float32)

    kept, sent = kept[:count], sent[:count]
    grad_low = jnp.where(core == 0, jnp.stack([kept, sent]), jnp.stack([sent, kept]))
    grad_hidden = jnp.einsum(
        "lsr,lfr->lsf", grad_low, factor_a, preferred_element_type=jnp.float32
    ).astype(jnp.bfloat16)
    grad_hidden = jnp.transpose(grad_hidden.reshape(2, CAP, sources, units), (0, 2, 1, 3))
    return grad_a, grad_b, grad_hidden[None], grad_gates


def solution(mesh):
    groups, sources = mesh.shape["dp"], mesh.shape["expert"]
    fine = Mesh(
        mesh.devices.reshape(groups // 2, 2, 2, sources // 2), ("q", "k", "x", "z")
    )
    dp = GROUPS
    tokens = P(("q", "k", "x", "z"), None)
    return jax.shard_map(
        body,
        mesh=fine,
        in_specs=(
            tokens,
            tokens,
            tokens,
            P(dp, EXPERT, None, None, None),
            P(EXPERT, None, None),
            P(EXPERT, None, None),
        ),
        out_specs=(
            P(EXPERT, dp, None),
            P(EXPERT, None, dp),
            P(dp, EXPERT, None, None, None),
            tokens,
        ),
        check_vma=False,
    )
```
